128 devices in a mesh: op: 8 (over x, core), sec: 16 (over z, y).
Axes of the slice: x: 4, y: 4, z: 4, core: 2. Of those that a mesh axis runs over, the one named last changes fastest.
Arguments:
- psi: bfloat16 [32, 16, 256, 256], P('sec'), may hold values from -6 to 6
- left_ops: bfloat16 [64, 32, 256, 256], P('op', 'sec'), may hold values from -0.375 to 0.375
- right_ops: bfloat16 [64, 16, 256, 256], P('op', 'sec'), may hold values from -0.046875 to 0.046875
- left_size: int32 [32], replicated, may hold values from 1 to 256, 6144 in all
- right_size: int32 [16], replicated, may hold values from 1 to 256, 3072 in all
- left_charge: int32 [32], replicated, may hold values from 0 to 4
- right_charge: int32 [16], replicated, may hold values from 0 to 4
Outputs:
- sigma: bfloat16 [32, 16, 256, 256], P(None, 'sec', 'op')
The draws below stay inside these ranges and needn't reach their ends.
Inputs may be any that keep to these rules, and one draw needn't show every extreme that they name: `left_size`: live rows of the left sectors sum to 6144. `right_size`: live columns of the right sectors sum to 3072.
All inputs are finite; a program needn't handle non-finite values.
Results may differ from the reference program's by a relative error of at most 0.0049.
Values may be sent and summed in bfloat16 or wider, within the bound.
A program may use at most 128 MiB of HBM per device.

```python
import math
import jax
import jax.numpy as jnp
import numpy as np
from jax import lax

BLK = 256
NA = 32
NB = 16
NOP = 64


def set_ends(values, stream_key, low, largest):
    dims = values.shape
    spot = [jax.random.randint(jax.random.fold_in(stream_key, axis), (), 0, dims[axis]) for axis in range(len(dims))]
    values = values.at[tuple(spot)].set(low)
    longest = dims.index(max(dims))
    spot[longest] = (spot[longest] + 1) % dims[longest]
    return values.at[tuple(spot)].set(largest)


def block_scale(own_key, shape, shards, least, high):
    def one(dim, blocks):
        heights = jax.random.uniform(jax.random.fold_in(jax.random.fold_in(own_key, 6), dim), (blocks,), jnp.float32, least / len(shards), high / len(shards))
        return jnp.repeat(jnp.exp(heights), shape[dim] // blocks).reshape((-1,) + (1,) * (len(shape) - dim - 1))

    loudness = one(*shards[0])
    for cut in shards[1:]:
        loudness = loudness * one(*cut)
    return loudness


def length_profile(amount, total, reach, skew):
    loads = [(1 << 20) // math.isqrt(grade ** skew) + 1 for grade in range(2, amount + 1)]
    spare, holding = total - reach - (amount - 1), [1] * (amount - 1)
    while spare > 0:
        free = [i for i in range(amount - 1) if holding[i] < reach]
        whole, remaining = sum([loads[i] for i in free]), spare
        for i in free:
            extra = min(reach - holding[i], max(1, remaining * loads[i] // whole), spare)
            holding[i] = holding[i] + extra
            spare = spare - extra
    return np.array([reach] + holding)


def uneven_parts(stream_key, count, total, most, lean):
    if count == 2:
        one = jax.random.randint(stream_key, (), max(1, total - most), min(most, total - 1) + 1)
        return jnp.stack([one, total - one])
    tallies = jnp.asarray(length_profile(count, total, most, lean), jnp.int32)
    couples = (count - 1) // 2
    giver, receiver = tallies[1:1 + 2 * couples:2], tallies[2:2 + 2 * couples:2]
    slack = jnp.minimum(giver - 1, most - receiver)
    shifted = jax.random.randint(jax.random.fold_in(stream_key, 1), (couples,), 0, 1 << 20) % (slack + 1)
    tallies = tallies.at[1:1 + 2 * couples:2].set(giver - shifted).at[2:2 + 2 * couples:2].set(receiver + shifted)
    return tallies[jax.random.permutation(jax.random.fold_in(stream_key, 2), count)]


def scatter_about(stream_key, dims, scale, most, split=(), kind=jnp.bfloat16):
    result = jax.random.normal(stream_key, dims, jnp.float32) * scale
    if len(split) > 0:
        result = block_scale(stream_key, dims, split, -0.22, 0.18) * result
    return jnp.clip(result, min=-most, max=most).astype(kind)


def setup_inputs(seed: int = 0) -> dict:
    key_of = jax.random.split(jax.random.key(seed), 8)
    psi = scatter_about(key_of[0], (NA, NB, BLK, BLK), 1.0, 6.0, ((0, 16),))
    left_ops = scatter_about(key_of[1], (NOP, NA, BLK, BLK), BLK ** -0.5, 0.375, ((0, 8), (1, 16)))
    right_ops = scatter_about(key_of[2], (NOP, NB, BLK, BLK), (BLK * NOP) ** -0.5, 0.046875, ((0, 8), (1, 16)))
    left_size = uneven_parts(key_of[3], NA, NA * 3 * BLK // 4, BLK, 1).astype(jnp.int32)
    right_size = uneven_parts(key_of[4], NB, NB * 3 * BLK // 4, BLK, 1).astype(jnp.int32)
    left_charge = set_ends(jax.random.randint(key_of[5], (NA,), 0, 5), jax.random.fold_in(key_of[5], 1), 0, 4).astype(jnp.int32)
    right_charge = set_ends(jax.random.randint(key_of[6], (NB,), 0, 5), jax.random.fold_in(key_of[6], 1), 0, 4).astype(jnp.int32)
    return {"psi": psi, "left_ops": left_ops, "right_ops": right_ops, "left_size": left_size, "right_size": right_size, "left_charge": left_charge, "right_charge": right_charge}


def build_mask(left_size, right_size, left_charge, right_charge):
    positions = jnp.arange(BLK, dtype=jnp.int32)
    allowed = jnp.abs(left_charge[:, None] - right_charge[None, :]) <= 1
    rows = positions[None, :] < left_size[:, None]
    cols = positions[None, :] < right_size[:, None]
    full = allowed[:, :, None, None] & rows[:, None, :, None] & cols[None, :, None, :]
    return full.astype(jnp.float32)


def reference(psi, left_ops, right_ops, left_size, right_size, left_charge, right_charge):
    mask = build_mask(left_size, right_size, left_charge, right_charge)
    masked = (psi.astype(jnp.float32) * mask).astype(jnp.bfloat16).astype(jnp.float32)

    def one_term(index, total):
        left = left_ops[index].astype(jnp.float32)
        right = right_ops[index].astype(jnp.float32)
        inner = jnp.einsum('aij,abjl->abil', left, masked).astype(jnp.bfloat16)
        inner = lax.optimization_barrier(inner).astype(jnp.float32)
        return total + jnp.einsum('abil,bml->abim', inner, right)

    total = lax.fori_loop(0, NOP, one_term, jnp.zeros(masked.shape, jnp.float32))
    return (total * mask).astype(jnp.bfloat16)
```

```python
import jax
import jax.numpy as jnp
from jax import lax
from jax.experimental import pallas as pl
from jax.experimental.pallas import tpu as pltpu
from jax.sharding import PartitionSpec as P

MESH = pl.DeviceIdType.MESH
BLK = 256
NK = 8
ROWS = 64


def wrap(i):
    return lax.rem(i, 4)


def kernel(lsize, rsize, lcharge, rcharge, psi, left, right, out,
           lb, rb, pb, pm, inner, stage, far, from_left, from_right, fin, got,
           own_sem, p1_send, p1_recv, px_send, px_recv, r_send, r_recv, l_send, l_recv,
           x_send, far_recv, x_recv, f_send, f_recv):
    op, sec = lax.axis_index("op"), lax.axis_index("sec")
    x, c = lax.div(op, 2), lax.rem(op, 2)
    z, y = lax.div(sec, 4), lax.rem(sec, 4)
    p, q = y + c * (z - y), z + c * (y - z)

    def sec_at(pp, qq):
        return 4 * qq + pp + 3 * c * (pp - qq)

    def dev(dx=0, dp=0, dq=0, other=False):
        core = 1 - c if other else c
        return (2 * wrap(x + dx) + core, sec_at(wrap(p + dp), wrap(q + dq)))

    def remote(src, dst, send, recv, to):
        return pltpu.make_async_remote_copy(src_ref=src, dst_ref=dst, send_sem=send, recv_sem=recv, device_id=to, device_id_type=MESH)

    barrier = pltpu.get_barrier_semaphore()
    senders = [dev(dp=s) for s in (1, 2, 3)] + [dev(dq=s) for s in (1, 2, 3)] + [dev(dx=s) for s in (1, 3)]
    senders += [dev(dp=s, other=True) for s in range(4)]
    for to in senders:
        pl.semaphore_signal(barrier, 1, device_id=to, device_id_type=MESH)

    own = [pltpu.make_async_copy(psi.at[:, sec_at(p, wrap(q + r))], pb.at[r, pl.ds(0, 2)], own_sem.at[r]) for r in range(4)]
    own += [pltpu.make_async_copy(right.at[k, 0], rb.at[0, :, pl.ds(k * BLK, BLK)], own_sem.at[4 + k]) for k in range(NK)]
    band = [wrap(x + d) for d in (2, 1, 3, 0)]
    for j in range(4):
        rows = pl.ds(pl.multiple_of(band[j] * ROWS, ROWS), ROWS)
        own += [pltpu.make_async_copy(left.at[:, a, rows], lb.at[j, a], own_sem.at[12 + 2 * j + a]) for a in range(2)]
    for copy in own:
        copy.start()

    pl.semaphore_wait(barrier, len(senders))

    sent = []

    def start(copy):
        copy.start()
        sent.append(copy)

    p1 = {s: remote(psi.at[:, sec_at(wrap(p + s), wrap(q + x))], pb.at[x, pl.ds(2 * (4 - s), 2)], p1_send.at[s - 1], p1_recv.at[3 - s], dev(dp=s))
          for s in (1, 2, 3)}
    for s in (1, 3, 2):
        start(p1[s])

    def r_copy(k, to_right):
        return remote(right.at[k, 0], rb.at[3 if to_right else 1, :, pl.ds(k * BLK, BLK)],
                      r_send.at[0 if to_right else 1, k], r_recv.at[2 if to_right else 0, k], dev(dq=1 if to_right else 3))

    def r_pass(k):
        here = rb.at[3 if k < 4 else 1, :, pl.ds(k * BLK, BLK)]
        return remote(here, rb.at[2, :, pl.ds(k * BLK, BLK)], r_send.at[2, k], r_recv.at[1, k], dev(dq=1 if k < 4 else 3))

    for i in range(NK):
        start(r_copy(i, True))
        start(r_copy(NK - 1 - i, False))

    def l_copy(j, a, to_right):
        rows = pl.ds(pl.multiple_of(band[j] * ROWS, ROWS), ROWS)
        slot = 3 if to_right else 1
        return remote(left.at[:, a, rows], lb.at[j, 2 * slot + a], l_send.at[j, 0 if to_right else 1, a], l_recv.at[j, slot - 1, a], dev(dp=1 if to_right else 3))

    def l_pass(j, a):
        here = lb.at[j, 2 * (3 if a == 0 else 1) + a]
        return remote(here, lb.at[j, 4 + a], l_send.at[j, 2, a], l_recv.at[j, 1, a], dev(dp=1 if a == 0 else 3))

    def l_start(j):
        for i in range(2):
            start(l_copy(j, i, True))
            start(l_copy(j, 1 - i, False))

    def l_forward(j):
        for i in range(2):
            l_copy(j, i, True).wait_recv()
            if i == 0:
                start(l_pass(j, 0))
            l_copy(j, 1 - i, False).wait_recv()
            if i == 0:
                start(l_pass(j, 1))

    for s in (1, 3, 2):
        p1[s].wait_recv()

    def px_part(slot_x, i):
        return pb.at[wrap(x + slot_x), pl.ds(2, 6)] if i is None else px_view(slot_x, i)

    def px_view(slot_x, half):
        return pb.at[wrap(x + slot_x), pl.ds(2 + 3 * half, 3)]

    def px_copy(half, to_right):
        return remote(px_view(0, half), px_view(0, half), px_send.at[0 if to_right else 1, half], px_recv.at[2 if to_right else 0, half],
                      dev(dx=1 if to_right else 3))

    def px_pass(half):
        slot_x = 3 if half == 0 else 1
        return remote(px_view(slot_x, half), px_view(slot_x, half), px_send.at[2, half], px_recv.at[1, half], dev(dx=1 if half == 0 else 3))

    def px_arrive(slot_x, half):
        return remote(px_view(slot_x, half), px_view(slot_x, half), px_send.at[2, half], px_recv.at[slot_x - 1, half], dev(dx=1))

    for i in range(2):
        start(px_copy(i, True))
        start(px_copy(1 - i, False))

    for i in range(4):
        r_copy(i, True).wait_recv()
        start(r_pass(i))
        r_copy(NK - 1 - i, False).wait_recv()
        start(r_pass(NK - 1 - i))
    l_start(0)
    px_arrive(3, 0).wait_recv()
    start(px_pass(0))
    px_arrive(1, 1).wait_recv()
    start(px_pass(1))
    l_start(1)
    for i in range(4, NK):
        r_copy(i, True).wait_recv()
        r_copy(NK - 1 - i, False).wait_recv()
    for copy in own:
        copy.wait()
    l_forward(0)
    for k in range(NK):
        r_pass(k).wait_recv()
    px_arrive(3, 1).wait_recv()
    px_arrive(1, 0).wait_recv()
    px_arrive(2, 0).wait_recv()
    px_arrive(2, 1).wait_recv()

    row_at = lax.broadcasted_iota(jnp.int32, (BLK, BLK), 0)
    col_at = lax.broadcasted_iota(jnp.int32, (BLK, BLK), 1)

    def mask_block(n, _):
        r, sa = lax.div(n, 8), lax.rem(n, 8)
        a = 2 * sec_at(wrap(p + lax.div(sa, 2)), q) + lax.rem(sa, 2)
        b = sec_at(p, wrap(q + r))
        live = (row_at < lsize[a]) & (col_at < rsize[b])
        block = pb[r, sa].astype(jnp.float32)
        pm[r, sa] = jnp.where(live, block, 0.0).astype(jnp.bfloat16)
        return 0

    lax.fori_loop(0, 32, mask_block, 0)

    def product(j, r):
        def first(sa, _):
            lhs = lb[j, sa].reshape(NK * ROWS, BLK)
            part = jnp.dot(lhs, pm[r, sa], preferred_element_type=jnp.float32).astype(jnp.bfloat16)
            here = pl.ds(pl.multiple_of(sa * ROWS, ROWS), ROWS)
            for k in range(NK):
                inner[here, k * BLK:(k + 1) * BLK] = part[k * ROWS:(k + 1) * ROWS]
            return 0

        lax.fori_loop(0, 8, first, 0)
        return lax.dot_general(inner[...], rb[r], (((1,), (1,)), ((), ())), preferred_element_type=jnp.float32)

    def far_copy(r):
        return remote(stage.at[0, r], far.at[r], x_send.at[0, r], far_recv.at[r], dev(dx=1 + 2 * lax.div(r, 2)))

    def x_copy(side, r):
        return remote(stage.at[1 + side, r], (from_left, from_right)[side].at[r], x_send.at[1 + side, r], x_recv.at[side, r], dev(dx=(1, 3)[side]))

    def fin_copy(r, other):
        core = 1 - c if other else c
        return remote(fin.at[r, core], got.at[c, wrap(4 - r)], f_send.at[r, 1 if other else 0], f_recv.at[c, wrap(4 - r)], dev(dq=r, other=other))

    def stage_far(n, _):
        r = 2 * lax.rem(n, 2) + lax.div(n, 2)
        stage[0, r] = product(0, r).astype(jnp.bfloat16)
        far_copy(r).start()
        return 0

    def stage_side(side):
        def body(n, _):
            r = wrap(n + 2) if side == 0 else n
            total = product(1 + side, r)

            @pl.when(n < 2)
            def _():
                stage[1 + side, r] = total.astype(jnp.bfloat16)

            @pl.when(n >= 2)
            def _():
                far_copy(r).wait_recv()
                stage[1 + side, r] = (total + far[r].astype(jnp.float32)).astype(jnp.bfloat16)

            x_copy(side, r).start()
            return 0

        return body

    def stage_own(n, _):
        r = wrap(n + 1)
        total = product(3, r)
        x_copy(0, r).wait_recv()
        x_copy(1, r).wait_recv()
        total = total + from_left[r].astype(jnp.float32) + from_right[r].astype(jnp.float32)
        total = total.astype(jnp.bfloat16).reshape(8, ROWS, BLK)
        fin[r, 0] = total[:, :32]
        fin[r, 1] = total[:, 32:]
        fin_copy(r, True).start()

        @pl.when(n < 3)
        def _():
            fin_copy(r, False).start()

        return 0

    bodies = [stage_far, stage_side(0), stage_side(1), stage_own]
    for j in range(4):
        if j < 3:
            l_forward(j + 1)
            if j < 2:
                l_start(j + 2)
        l_pass(j, 0).wait_recv()
        l_pass(j, 1).wait_recv()
        lax.fori_loop(0, 4, bodies[j], 0)

    got[c, 0] = fin[0, c]

    def arrived(part, slot):
        return remote(fin.at[0, 0], got.at[part, slot], f_send.at[0, 0], f_recv.at[part, slot], dev(dq=1))

    for s in range(4):
        arrived(1 - c, s).wait_recv()
    for s in range(1, 4):
        arrived(c, s).wait_recv()

    row_at = lax.broadcasted_iota(jnp.int32, (32, BLK), 0) + 32 * op
    col_live = lax.broadcasted_iota(jnp.int32, (32, BLK), 1) < rsize[sec]

    def finish(n, _):
        sz, sy, i = lax.div(n, 8), lax.rem(lax.div(n, 2), 4), lax.rem(n, 2)
        a = 2 * (4 * wrap(z + sz) + wrap(y + sy)) + i
        total = got[0, sz, 2 * sy + i].astype(jnp.float32) + got[1, sy, 2 * sz + i].astype(jnp.float32)
        rows = jnp.where(jnp.abs(lcharge[a] - rcharge[sec]) <= 1, lsize[a], 0)
        out[a] = jnp.where((row_at < rows) & col_live, total, 0.0).astype(jnp.bfloat16)
        return 0

    lax.fori_loop(0, 32, finish, 0)

    for copy in sent:
        copy.wait_send()

    def drain(r, _):
        far_copy(r).wait_send()
        x_copy(0, r).wait_send()
        x_copy(1, r).wait_send()
        fin_copy(r, True).wait_send()
        return 0

    lax.fori_loop(0, 4, drain, 0)
    for r in range(1, 4):
        fin_copy(r, False).wait_send()


def per_device(psi, left_ops, right_ops, left_size, right_size, left_charge, right_charge):
    smem = pl.BlockSpec(memory_space=pltpu.SMEM)
    hbm = pl.BlockSpec(memory_space=pl.ANY)
    dma = pltpu.SemaphoreType.DMA
    band = (8, ROWS, BLK)
    result = pl.pallas_call(
        kernel,
        out_shape=jax.ShapeDtypeStruct((32, 32, BLK), jnp.bfloat16),
        in_specs=[smem] * 4 + [hbm] * 3,
        out_specs=pl.BlockSpec(memory_space=pltpu.VMEM),
        scratch_shapes=[
            pltpu.VMEM((4, 8, NK, ROWS, BLK), jnp.bfloat16),
            pltpu.VMEM((4, BLK, NK * BLK), jnp.bfloat16),
            pltpu.VMEM((4, 8, BLK, BLK), jnp.bfloat16),
            pltpu.VMEM((4, 8, BLK, BLK), jnp.bfloat16),
            pltpu.VMEM((8 * ROWS, NK * BLK), jnp.bfloat16),
            pltpu.VMEM((3, 4, 8 * ROWS, BLK), jnp.bfloat16),
            pltpu.VMEM((4, 8 * ROWS, BLK), jnp.bfloat16),
            pltpu.VMEM((4, 8 * ROWS, BLK), jnp.bfloat16),
            pltpu.VMEM((4, 8 * ROWS, BLK), jnp.bfloat16),
            pltpu.VMEM((4, 2, 8, 32, BLK), jnp.bfloat16),
            pltpu.VMEM((2, 4, 8, 32, BLK), jnp.bfloat16),
            dma((20,)), dma((3,)), dma((3,)), dma((3, 2)), dma((3, 2)), dma((3, NK)), dma((3, NK)),
            dma((4, 3, 2)), dma((4, 3, 2)), dma((3, 4)), dma((4,)), dma((2, 4)), dma((4, 2)), dma((2, 4)),
        ],
        compiler_params=pltpu.CompilerParams(collective_id=0, has_side_effects=True, vmem_limit_bytes=56 * 2**20),
        cost_estimate=pl.CostEstimate(flops=17_200_000_000, bytes_accessed=8_000_000, transcendentals=0),
    )(left_size, right_size, left_charge, right_charge, psi, left_ops, right_ops)
    return result[:, None]


def solution(mesh):
    in_specs = (P("sec", None, None, None), P("op", "sec", None, None), P("op", "sec", None, None), P(), P(), P(), P())
    return jax.shard_map(per_device, mesh=mesh, in_specs=in_specs, out_specs=P(None, "sec", "op", None), check_vma=False)
```

```python
import jax
import jax.numpy as jnp
from jax import lax
from jax.experimental import pallas as pl
from jax.experimental.pallas import tpu as pltpu
from jax.sharding import PartitionSpec as P

MESH = pl.DeviceIdType.MESH
BLK = 256
NK = 8
ROWS = 64
HALF = 32
UNROLL = 4


def wrap(i):
    return lax.rem(i, 4)


def kernel(lsize, rsize, lcharge, rcharge, psi, left, right, out,
           lb, rb, pb, pm, inner, stage, far, near, mine, fin, got,
           own_sem, p_send, p_recv, px_send, px_recv, r_send, r_recv, l_send, l_recv,
           x_send, far_recv, x_recv, f_send, f_recv):
    op, sec = lax.axis_index("op"), lax.axis_index("sec")
    x, c = lax.div(op, 2), lax.rem(op, 2)
    z, y = lax.div(sec, 4), lax.rem(sec, 4)
    p, q = y + c * (z - y), z + c * (y - z)

    def sec_at(pp, qq):
        return 4 * qq + pp + 3 * c * (pp - qq)

    def dev(dx=0, dp=0, dq=0, other=False):
        core = 1 - c if other else c
        return (2 * wrap(x + dx) + core, sec_at(wrap(p + dp), wrap(q + dq)))

    def remote(src, dst, send, recv, to):
        return pltpu.make_async_remote_copy(src_ref=src, dst_ref=dst, send_sem=send, recv_sem=recv, device_id=to, device_id_type=MESH)

    barrier = pltpu.get_barrier_semaphore()
    senders = [dev(dp=s) for s in (1, 2, 3)] + [dev(dq=s) for s in (1, 2, 3)] + [dev(dx=s) for s in (1, 3)]
    senders += [dev(dp=s, other=True) for s in range(4)]
    for to in senders:
        pl.semaphore_signal(barrier, 1, device_id=to, device_id_type=MESH)

    def start_row(j, half):
        place = (wrap(x + 2) * ROWS + HALF * half, wrap(x + 1 + 2 * half) * ROWS + HALF * (1 - half), wrap(x + 1 + 2 * half) * ROWS + HALF * half, x * ROWS + HALF * half)[j]
        return pl.ds(pl.multiple_of(place, HALF), HALF)

    def half_rows(half):
        return pl.ds(HALF * half, HALF)

    own = [pltpu.make_async_copy(psi.at[:, sec_at(p, wrap(q + r))], pb.at[r, pl.ds(0, 2)], own_sem.at[r]) for r in range(4)]
    own += [pltpu.make_async_copy(right.at[k, 0], rb.at[0, :, pl.ds(k * BLK, BLK)], own_sem.at[4 + k]) for k in range(NK)]
    for j in range(4):
        for a in range(2):
            for h in range(2):
                own.append(pltpu.make_async_copy(left.at[:, a, start_row(j, h)], lb.at[j, a, :, half_rows(h)], own_sem.at[12 + 4 * j + 2 * a + h]))
    for copy in own:
        copy.start()

    pl.semaphore_wait(barrier, len(senders))

    sent = []

    def start(copy):
        copy.start()
        sent.append(copy)

    quarter = pl.ds(pl.multiple_of(x * ROWS, ROWS), ROWS)

    def p_copy(s, r):
        b = sec_at(wrap(p + s), wrap(q + r))
        if r == 0:
            return remote(psi.at[:, b], pb.at[0, pl.ds(2 * (4 - s), 2)], p_send.at[s - 1, 0], p_recv.at[3 - s, 0], dev(dp=s))
        return remote(psi.at[:, b, quarter], pb.at[r, pl.ds(2 * (4 - s), 2), quarter], p_send.at[s - 1, r], p_recv.at[3 - s, r], dev(dp=s))

    def r_copy(k, to_right):
        return remote(right.at[k, 0], rb.at[3 if to_right else 1, :, pl.ds(k * BLK, BLK)],
                      r_send.at[0 if to_right else 1, k], r_recv.at[2 if to_right else 0, k], dev(dq=1 if to_right else 3))

    def r_pass(k):
        here = rb.at[3 if k < 4 else 1, :, pl.ds(k * BLK, BLK)]
        return remote(here, rb.at[2, :, pl.ds(k * BLK, BLK)], r_send.at[2, k], r_recv.at[1, k], dev(dq=1 if k < 4 else 3))

    def l_copy(j, a, h, to_right):
        slot = 3 if to_right else 1
        return remote(left.at[:, a, start_row(j, h)], lb.at[j, 2 * slot + a, :, half_rows(h)],
                      l_send.at[j, 0 if to_right else 1, a, h], l_recv.at[j, slot - 1, a, h], dev(dp=1 if to_right else 3))

    def l_pass(j, a):
        here = lb.at[j, 2 * (3 if a == 0 else 1) + a]
        return remote(here, lb.at[j, 4 + a], l_send.at[j, 2, a, 0], l_recv.at[j, 1, a, 0], dev(dp=1 if a == 0 else 3))

    def l_start(j):
        for i in range(2):
            for h in range(2):
                start(l_copy(j, i, h, True))
                start(l_copy(j, 1 - i, h, False))

    def l_forward(j):
        for i in range(2):
            for h in range(2):
                l_copy(j, i, h, True).wait_recv()
            if i == 0:
                start(l_pass(j, 0))
            for h in range(2):
                l_copy(j, 1 - i, h, False).wait_recv()
            if i == 0:
                start(l_pass(j, 1))

    def px_view(slot_x, half):
        return pb.at[pl.ds(1, 3), pl.ds(2 + 3 * half, 3), pl.ds(pl.multiple_of(wrap(x + slot_x) * ROWS, ROWS), ROWS)]

    def px_copy(half, to_right):
        return remote(px_view(0, half), px_view(0, half), px_send.at[0 if to_right else 1, half], px_recv.at[2 if to_right else 0, half],
                      dev(dx=1 if to_right else 3))

    def px_pass(half):
        slot_x = 3 if half == 0 else 1
        return remote(px_view(slot_x, half), px_view(slot_x, half), px_send.at[2, half], px_recv.at[1, half], dev(dx=1 if half == 0 else 3))

    def px_arrive(slot_x, half):
        return remote(px_view(slot_x, half), px_view(slot_x, half), px_send.at[2, half], px_recv.at[slot_x - 1, half], dev(dx=1))

    row_at = lax.broadcasted_iota(jnp.int32, (BLK, BLK), 0)
    col_at = lax.broadcasted_iota(jnp.int32, (BLK, BLK), 1)

    def mask_block(n, _):
        r, sa = lax.div(n, 8), lax.rem(n, 8)
        a = 2 * sec_at(wrap(p + lax.div(sa, 2)), q) + lax.rem(sa, 2)
        b = sec_at(p, wrap(q + r))
        live = (row_at < lsize[a]) & (col_at < rsize[b])
        block = pb[r, sa].astype(jnp.float32)
        pm[r, sa] = jnp.where(live, block, 0.0).astype(jnp.bfloat16)
        return 0

    def product(j, r):
        def first(sa, _):
            lhs = lb[j, sa].reshape(NK * ROWS, BLK)
            part = jnp.dot(lhs, pm[r, sa], preferred_element_type=jnp.float32).astype(jnp.bfloat16)
            here = pl.ds(pl.multiple_of(sa * ROWS, ROWS), ROWS)
            for k in range(NK):
                inner[here, k * BLK:(k + 1) * BLK] = part[k * ROWS:(k + 1) * ROWS]
            return 0

        lax.fori_loop(0, 8, first, 0, unroll=UNROLL)
        total = lax.dot_general(inner[...], rb[r], (((1,), (1,)), ((), ())), preferred_element_type=jnp.float32)
        return total.reshape(8, ROWS, BLK)

    def far_copy(side, r):
        return remote(stage.at[0, side, r], far.at[side, r], x_send.at[0, side, r], far_recv.at[side, r], dev(dx=(1, 3)[side]))

    def x_copy(j, side, r):
        return remote(stage.at[j, side, r], near.at[j - 1, side, r], x_send.at[j, side, r], x_recv.at[j - 1, side, r], dev(dx=(1, 3)[side]))

    def fin_copy(r, other):
        core = 1 - c if other else c
        return remote(fin.at[r, core], got.at[c, wrap(4 - r)], f_send.at[r, 1 if other else 0], f_recv.at[c, wrap(4 - r)], dev(dq=r, other=other))

    def halves(total):
        return total[:, :HALF], total[:, HALF:]

    def stage_far(r):
        for side, part in enumerate(halves(product(0, r))):
            stage[0, side, r] = part.astype(jnp.bfloat16)
            far_copy(side, r).start()

    def stage_one(r):
        for side, part in enumerate(halves(product(1, r))):
            stage[1, side, r] = part.astype(jnp.bfloat16)
            x_copy(1, side, r).start()

    def stage_two(r):
        parts = halves(product(2, r))
        for side in range(2):
            far_copy(side, r).wait_recv()
            stage[2, side, r] = (parts[side] + far[side, r].astype(jnp.float32)).astype(jnp.bfloat16)
            x_copy(2, side, r).start()

    def stage_own(r):
        mine[r] = product(3, r)

    def slot_order(n):
        return n + lax.div(n, 2) * (5 - 2 * n)

    def run(body, low):
        def step(n, _):
            body(slot_order(n))
            return 0

        lax.fori_loop(low, 4, step, 0)

    for s in (1, 3, 2):
        for r in (1, 2, 3):
            start(p_copy(s, r))
    for s in (1, 3, 2):
        start(p_copy(s, 0))
    l_start(0)
    for i in range(NK):
        start(r_copy(i, True))
        start(r_copy(NK - 1 - i, False))
    for s in (1, 3, 2):
        for r in (1, 2, 3):
            p_copy(s, r).wait_recv()
    for i in range(2):
        start(px_copy(i, True))
        start(px_copy(1 - i, False))
    for copy in own:
        copy.wait()
    for s in (1, 3, 2):
        p_copy(s, 0).wait_recv()
    lax.fori_loop(0, 8, mask_block, 0)
    l_forward(0)
    px_arrive(3, 0).wait_recv()
    start(px_pass(0))
    px_arrive(1, 1).wait_recv()
    start(px_pass(1))
    for i in range(4):
        r_copy(i, True).wait_recv()
        start(r_pass(i))
        r_copy(NK - 1 - i, False).wait_recv()
        start(r_pass(NK - 1 - i))
    l_start(1)
    l_pass(0, 0).wait_recv()
    l_pass(0, 1).wait_recv()
    stage_far(0)
    px_arrive(3, 1).wait_recv()
    px_arrive(1, 0).wait_recv()
    px_arrive(2, 0).wait_recv()
    px_arrive(2, 1).wait_recv()
    lax.fori_loop(8, 32, mask_block, 0)
    for i in range(4, NK):
        r_copy(i, True).wait_recv()
        r_copy(NK - 1 - i, False).wait_recv()
    l_start(2)
    for k in range(NK):
        r_pass(k).wait_recv()
    run(stage_far, 1)
    l_forward(1)
    l_start(3)
    for j, body in ((1, stage_one), (2, stage_two), (3, stage_own)):
        if j < 3:
            l_forward(j + 1)
        l_pass(j, 0).wait_recv()
        l_pass(j, 1).wait_recv()
        run(body, 0)

    def close(r):
        for h in range(2):
            x_copy(2 - h, 0, r).wait_recv()
            x_copy(1 + h, 1, r).wait_recv()
            total = mine[r, :, HALF * h:HALF * (h + 1)] + near[1 - h, 0, r].astype(jnp.float32) + near[h, 1, r].astype(jnp.float32)
            fin[r, h] = total.astype(jnp.bfloat16)
        fin_copy(r, True).start()

        @pl.when(r > 0)
        def _():
            fin_copy(r, False).start()

    run(close, 0)

    got[c, 0] = fin[0, c]

    def arrived(part, slot):
        return remote(fin.at[0, 0], got.at[part, slot], f_send.at[0, 0], f_recv.at[part, slot], dev(dq=1))

    for s in range(4):
        arrived(1 - c, s).wait_recv()
    for s in range(1, 4):
        arrived(c, s).wait_recv()

    row_at = lax.broadcasted_iota(jnp.int32, (32, BLK), 0) + 32 * op
    col_live = lax.broadcasted_iota(jnp.int32, (32, BLK), 1) < rsize[sec]

    def finish(n, _):
        sz, sy, i = lax.div(n, 8), lax.rem(lax.div(n, 2), 4), lax.rem(n, 2)
        a = 2 * (4 * wrap(z + sz) + wrap(y + sy)) + i
        total = got[0, sz, 2 * sy + i].astype(jnp.float32) + got[1, sy, 2 * sz + i].astype(jnp.float32)
        rows = jnp.where(jnp.abs(lcharge[a] - rcharge[sec]) <= 1, lsize[a], 0)
        out[a] = jnp.where((row_at < rows) & col_live, total, 0.0).astype(jnp.bfloat16)
        return 0

    lax.fori_loop(0, 32, finish, 0)

    for copy in sent:
        copy.wait_send()

    def drain(r, _):
        for side in range(2):
            far_copy(side, r).wait_send()
            x_copy(1, side, r).wait_send()
            x_copy(2, side, r).wait_send()
        fin_copy(r, True).wait_send()
        return 0

    lax.fori_loop(0, 4, drain, 0)
    for r in range(1, 4):
        fin_copy(r, False).wait_send()


def per_device(psi, left_ops, right_ops, left_size, right_size, left_charge, right_charge):
    smem = pl.BlockSpec(memory_space=pltpu.SMEM)
    hbm = pl.BlockSpec(memory_space=pl.ANY)
    dma = pltpu.SemaphoreType.DMA
    result = pl.pallas_call(
        kernel,
        out_shape=jax.ShapeDtypeStruct((32, 32, BLK), jnp.bfloat16),
        in_specs=[smem] * 4 + [hbm] * 3,
        out_specs=pl.BlockSpec(memory_space=pltpu.VMEM),
        scratch_shapes=[
            pltpu.VMEM((4, 8, NK, ROWS, BLK), jnp.bfloat16),
            pltpu.VMEM((4, BLK, NK * BLK), jnp.bfloat16),
            pltpu.VMEM((4, 8, BLK, BLK), jnp.bfloat16),
            pltpu.VMEM((4, 8, BLK, BLK), jnp.bfloat16),
            pltpu.VMEM((8 * ROWS, NK * BLK), jnp.bfloat16),
            pltpu.VMEM((3, 2, 4, 8, HALF, BLK), jnp.bfloat16),
            pltpu.VMEM((2, 4, 8, HALF, BLK), jnp.bfloat16),
            pltpu.VMEM((2, 2, 4, 8, HALF, BLK), jnp.bfloat16),
            pltpu.VMEM((4, 8, ROWS, BLK), jnp.float32),
            pltpu.VMEM((4, 2, 8, HALF, BLK), jnp.bfloat16),
            pltpu.VMEM((2, 4, 8, HALF, BLK), jnp.bfloat16),
            dma((28,)), dma((3, 4)), dma((3, 4)), dma((3, 2)), dma((3, 2)), dma((3, NK)), dma((3, NK)),
            dma((4, 3, 2, 2)), dma((4, 3, 2, 2)), dma((3, 2, 4)), dma((2, 4)), dma((2, 2, 4)), dma((4, 2)), dma((2, 4)),
        ],
        compiler_params=pltpu.CompilerParams(collective_id=0, has_side_effects=True, vmem_limit_bytes=56 * 2**20),
        cost_estimate=pl.CostEstimate(flops=17_200_000_000, bytes_accessed=8_000_000, transcendentals=0),
    )(left_size, right_size, left_charge, right_charge, psi, left_ops, right_ops)
    return result[:, None]


def solution(mesh):
    in_specs = (P("sec", None, None, None), P("op", "sec", None, None), P("op", "sec", None, None), P(), P(), P(), P())
    return jax.shard_map(per_device, mesh=mesh, in_specs=in_specs, out_specs=P(None, "sec", "op", None), check_vma=False)
```

```python
import jax
import jax.numpy as jnp
from jax import lax
from jax.experimental import pallas as pl
from jax.experimental.pallas import tpu as pltpu
from jax.sharding import PartitionSpec as P

MESH = pl.DeviceIdType.MESH
BLK = 256
NK = 8
ROWS = 64
HALF = 32


def wrap(i):
    return lax.rem(i, 4)


def kernel(lsize, rsize, lcharge, rcharge, psi, left, right, out,
           lb, rb, pb, pm, inner, stage, far, near, mine, fin, got,
           own_sem, p_send, p_recv, px_send, px_recv, r_send, r_recv, l_send, l_recv,
           x_send, far_recv, x_recv, f_send, f_recv):
    op, sec = lax.axis_index("op"), lax.axis_index("sec")
    x, c = lax.div(op, 2), lax.rem(op, 2)
    z, y = lax.div(sec, 4), lax.rem(sec, 4)
    p, q = y + c * (z - y), z + c * (y - z)

    def sec_at(pp, qq):
        return 4 * qq + pp + 3 * c * (pp - qq)

    def dev(dx=0, dp=0, dq=0, other=False):
        core = 1 - c if other else c
        return (2 * wrap(x + dx) + core, sec_at(wrap(p + dp), wrap(q + dq)))

    def remote(src, dst, send, recv, to):
        return pltpu.make_async_remote_copy(src_ref=src, dst_ref=dst, send_sem=send, recv_sem=recv, device_id=to, device_id_type=MESH)

    barrier = pltpu.get_barrier_semaphore()
    senders = [dev(dp=s) for s in (1, 2, 3)] + [dev(dq=s) for s in (1, 2, 3)] + [dev(dx=s) for s in (1, 3)]
    senders += [dev(dp=s, other=True) for s in range(4)]
    for to in senders:
        pl.semaphore_signal(barrier, 1, device_id=to, device_id_type=MESH)

    def start_row(j, half):
        place = (wrap(x + 2) * ROWS + HALF * half, wrap(x + 1 + 2 * half) * ROWS + HALF * (1 - half), wrap(x + 1 + 2 * half) * ROWS + HALF * half, x * ROWS + HALF * half)[j]
        return pl.ds(pl.multiple_of(place, HALF), HALF)

    def half_rows(half):
        return pl.ds(HALF * half, HALF)

    own = [pltpu.make_async_copy(psi.at[:, sec_at(p, wrap(q + r))], pb.at[r, pl.ds(0, 2)], own_sem.at[r]) for r in range(4)]
    own += [pltpu.make_async_copy(right.at[k, 0], rb.at[0, :, pl.ds(k * BLK, BLK)], own_sem.at[4 + k]) for k in range(NK)]
    for j in range(4):
        for a in range(2):
            for h in range(2):
                own.append(pltpu.make_async_copy(left.at[:, a, start_row(j, h)], lb.at[j, a, :, half_rows(h)], own_sem.at[12 + 4 * j + 2 * a + h]))
    for copy in own:
        copy.start()

    pl.semaphore_wait(barrier, len(senders))

    sent = []

    def start(copy):
        copy.start()
        sent.append(copy)

    def p_copy(s):
        return remote(psi.at[:, sec_at(wrap(p + s), wrap(q + x))], pb.at[x, pl.ds(2 * (4 - s), 2)], p_send.at[s - 1], p_recv.at[3 - s], dev(dp=s))

    def r_copy(k, to_right):
        return remote(right.at[k, 0], rb.at[3 if to_right else 1, :, pl.ds(k * BLK, BLK)],
                      r_send.at[0 if to_right else 1, k], r_recv.at[2 if to_right else 0, k], dev(dq=1 if to_right else 3))

    def r_pass(k):
        here = rb.at[3 if k < 4 else 1, :, pl.ds(k * BLK, BLK)]
        return remote(here, rb.at[2, :, pl.ds(k * BLK, BLK)], r_send.at[2, k], r_recv.at[1, k], dev(dq=1 if k < 4 else 3))

    def l_copy(j, a, h, to_right):
        slot = 3 if to_right else 1
        return remote(left.at[:, a, start_row(j, h)], lb.at[j, 2 * slot + a, :, half_rows(h)],
                      l_send.at[j, 0 if to_right else 1, a, h], l_recv.at[j, slot - 1, a, h], dev(dp=1 if to_right else 3))

    def l_pass(j, a):
        here = lb.at[j, 2 * (3 if a == 0 else 1) + a]
        return remote(here, lb.at[j, 4 + a], l_send.at[j, 2, a, 0], l_recv.at[j, 1, a, 0], dev(dp=1 if a == 0 else 3))

    def l_start(j):
        for i in range(2):
            for h in range(2):
                start(l_copy(j, i, h, True))
                start(l_copy(j, 1 - i, h, False))

    def l_forward(j):
        for i in range(2):
            for h in range(2):
                l_copy(j, i, h, True).wait_recv()
            if i == 0:
                start(l_pass(j, 0))
            for h in range(2):
                l_copy(j, 1 - i, h, False).wait_recv()
            if i == 0:
                start(l_pass(j, 1))

    def px_view(slot_x, piece):
        return pb.at[wrap(x + slot_x), pl.ds((2, 6, 4, 5)[piece], 2 if piece < 2 else 1)]

    def px_copy(piece, to_right):
        return remote(px_view(0, piece), px_view(0, piece), px_send.at[0 if to_right else 1, piece], px_recv.at[2 if to_right else 0, piece],
                      dev(dx=1 if to_right else 3))

    def px_pass(piece):
        slot_x = 3 if piece % 2 == 0 else 1
        return remote(px_view(slot_x, piece), px_view(slot_x, piece), px_send.at[2, piece], px_recv.at[1, piece], dev(dx=1 if piece % 2 == 0 else 3))

    def px_arrive(slot_x, piece):
        return remote(px_view(slot_x, piece), px_view(slot_x, piece), px_send.at[2, piece], px_recv.at[slot_x - 1, piece], dev(dx=1))

    row_at = lax.broadcasted_iota(jnp.int32, (BLK, BLK), 0)
    col_at = lax.broadcasted_iota(jnp.int32, (BLK, BLK), 1)

    def mask_slot(d):
        lax.fori_loop(0, 8, lambda sa, _: mask_block(wrap(x + d), sa), 0)

    def mask_block(r, sa):
        a = 2 * sec_at(wrap(p + lax.div(sa, 2)), q) + lax.rem(sa, 2)
        b = sec_at(p, wrap(q + r))
        live = (row_at < lsize[a]) & (col_at < rsize[b])
        block = pb[r, sa].astype(jnp.float32)
        pm[r, sa] = jnp.where(live, block, 0.0).astype(jnp.bfloat16)
        return 0

    def slot_order(n):
        return n + lax.div(n, 2) * (5 - 2 * n)

    def first(j, sectors, begin=0, end=4):
        def step(n, _):
            r = wrap(x + slot_order(n))
            for sa in sectors:
                lhs = lb[j, sa].reshape(NK * ROWS, BLK)
                part = jnp.dot(lhs, pm[r, sa], preferred_element_type=jnp.float32).astype(jnp.bfloat16)
                for k in range(NK):
                    inner[r, sa * ROWS:(sa + 1) * ROWS, k * BLK:(k + 1) * BLK] = part[k * ROWS:(k + 1) * ROWS]
            return 0

        lax.fori_loop(begin, end, step, 0)

    def product(r):
        total = lax.dot_general(inner[r], rb[r], (((1,), (1,)), ((), ())), preferred_element_type=jnp.float32)
        return total.reshape(8, ROWS, BLK)

    def far_copy(side, r):
        return remote(stage.at[0, side, r], far.at[side, r], x_send.at[0, side, r], far_recv.at[side, r], dev(dx=(1, 3)[side]))

    def x_copy(j, side, r):
        return remote(stage.at[j, side, r], near.at[j - 1, side, r], x_send.at[j, side, r], x_recv.at[j - 1, side, r], dev(dx=(1, 3)[side]))

    def fin_copy(r, other):
        core = 1 - c if other else c
        return remote(fin.at[r, core], got.at[c, wrap(4 - r)], f_send.at[r, 1 if other else 0], f_recv.at[c, wrap(4 - r)], dev(dq=r, other=other))

    def halves(total):
        return total[:, :HALF], total[:, HALF:]

    def stage_far(r):
        for side, part in enumerate(halves(product(r))):
            stage[0, side, r] = part.astype(jnp.bfloat16)
            far_copy(side, r).start()

    def stage_one(r):
        for side, part in enumerate(halves(product(r))):
            stage[1, side, r] = part.astype(jnp.bfloat16)
            x_copy(1, side, r).start()

    def stage_two(r):
        parts = halves(product(r))
        for side in range(2):
            far_copy(side, r).wait_recv()
            stage[2, side, r] = (parts[side] + far[side, r].astype(jnp.float32)).astype(jnp.bfloat16)
            x_copy(2, side, r).start()

    def stage_own(r):
        mine[r] = product(r)

    def run(body, low, high, down=False):
        def step(n, _):
            body(3 - n if down else wrap(x + slot_order(n)))
            return 0

        lax.fori_loop(low, high, step, 0)

    for s in (1, 3, 2):
        start(p_copy(s))
    for s in (1, 3):
        p_copy(s).wait_recv()
    for piece in range(2):
        start(px_copy(piece, True))
        start(px_copy(1 - piece, False))
    for i in range(NK):
        start(r_copy(i, True))
        start(r_copy(NK - 1 - i, False))
    p_copy(2).wait_recv()
    for piece in range(2, 4):
        start(px_copy(piece, True))
        start(px_copy(5 - piece, False))
    for copy in own:
        copy.wait()
    mask_slot(0)
    for i in range(4):
        r_copy(i, True).wait_recv()
        start(r_pass(i))
        r_copy(NK - 1 - i, False).wait_recv()
        start(r_pass(NK - 1 - i))
    l_start(0)
    for piece in (0, 1):
        px_arrive(3 - 2 * (piece % 2), piece).wait_recv()
        start(px_pass(piece))
    for piece in (2, 3):
        px_arrive(3 - 2 * (piece % 2), piece).wait_recv()
        start(px_pass(piece))
    for i in range(4, NK):
        r_copy(i, True).wait_recv()
        r_copy(NK - 1 - i, False).wait_recv()
    l_forward(0)
    l_start(1)
    for piece in range(4):
        px_arrive(1 + 2 * (piece % 2), piece).wait_recv()
    mask_slot(1)
    mask_slot(3)
    first(0, (0, 1, 2, 3, 6, 7), 0, 3)
    l_pass(0, 0).wait_recv()
    l_pass(0, 1).wait_recv()
    first(0, (4, 5), 0, 3)
    for k in range(NK):
        r_pass(k).wait_recv()
    l_forward(1)
    l_start(2)
    run(stage_far, 0, 3)
    for piece in range(4):
        px_arrive(2, piece).wait_recv()
    mask_slot(2)
    first(0, range(8), 3, 4)
    run(stage_far, 3, 4)
    first(1, (0, 1, 2, 3, 6, 7))
    l_pass(1, 0).wait_recv()
    l_pass(1, 1).wait_recv()
    first(1, (4, 5))
    l_forward(2)
    l_start(3)
    run(stage_one, 0, 4)
    first(2, (0, 1, 2, 3, 6, 7))
    l_pass(2, 0).wait_recv()
    l_pass(2, 1).wait_recv()
    first(2, (4, 5))
    l_forward(3)
    run(stage_two, 0, 4, True)
    first(3, (0, 1, 2, 3, 6, 7))
    l_pass(3, 0).wait_recv()
    l_pass(3, 1).wait_recv()
    first(3, (4, 5))
    run(stage_own, 0, 4)

    def close(r):
        for h in range(2):
            x_copy(2 - h, 0, r).wait_recv()
            x_copy(1 + h, 1, r).wait_recv()
            total = mine[r, :, HALF * h:HALF * (h + 1)] + near[1 - h, 0, r].astype(jnp.float32) + near[h, 1, r].astype(jnp.float32)
            fin[r, h] = total.astype(jnp.bfloat16)
        fin_copy(r, True).start()

        @pl.when(r > 0)
        def _():
            fin_copy(r, False).start()

    run(close, 0, 4, True)

    got[c, 0] = fin[0, c]

    def arrived(part, slot):
        return remote(fin.at[0, 0], got.at[part, slot], f_send.at[0, 0], f_recv.at[part, slot], dev(dq=1))

    for s in range(4):
        arrived(1 - c, s).wait_recv()
    for s in range(1, 4):
        arrived(c, s).wait_recv()

    row_at = lax.broadcasted_iota(jnp.int32, (32, BLK), 0) + 32 * op
    col_live = lax.broadcasted_iota(jnp.int32, (32, BLK), 1) < rsize[sec]

    def finish(n, _):
        sz, sy, i = lax.div(n, 8), lax.rem(lax.div(n, 2), 4), lax.rem(n, 2)
        a = 2 * (4 * wrap(z + sz) + wrap(y + sy)) + i
        total = got[0, sz, 2 * sy + i].astype(jnp.float32) + got[1, sy, 2 * sz + i].astype(jnp.float32)
        rows = jnp.where(jnp.abs(lcharge[a] - rcharge[sec]) <= 1, lsize[a], 0)
        out[a] = jnp.where((row_at < rows) & col_live, total, 0.0).astype(jnp.bfloat16)
        return 0

    lax.fori_loop(0, 32, finish, 0)

    for copy in sent:
        copy.wait_send()

    def drain(r, _):
        for side in range(2):
            far_copy(side, r).wait_send()
            x_copy(1, side, r).wait_send()
            x_copy(2, side, r).wait_send()
        fin_copy(r, True).wait_send()
        return 0

    lax.fori_loop(0, 4, drain, 0)
    for r in range(1, 4):
        fin_copy(r, False).wait_send()


def per_device(psi, left_ops, right_ops, left_size, right_size, left_charge, right_charge):
    smem = pl.BlockSpec(memory_space=pltpu.SMEM)
    hbm = pl.BlockSpec(memory_space=pl.ANY)
    dma = pltpu.SemaphoreType.DMA
    result = pl.pallas_call(
        kernel,
        out_shape=jax.ShapeDtypeStruct((32, 32, BLK), jnp.bfloat16),
        in_specs=[smem] * 4 + [hbm] * 3,
        out_specs=pl.BlockSpec(memory_space=pltpu.VMEM),
        scratch_shapes=[
            pltpu.VMEM((4, 8, NK, ROWS, BLK), jnp.bfloat16),
            pltpu.VMEM((4, BLK, NK * BLK), jnp.bfloat16),
            pltpu.VMEM((4, 8, BLK, BLK), jnp.bfloat16),
            pltpu.VMEM((4, 8, BLK, BLK), jnp.bfloat16),
            pltpu.VMEM((4, 8 * ROWS, NK * BLK), jnp.bfloat16),
            pltpu.VMEM((3, 2, 4, 8, HALF, BLK), jnp.bfloat16),
            pltpu.VMEM((2, 4, 8, HALF, BLK), jnp.bfloat16),
            pltpu.VMEM((2, 2, 4, 8, HALF, BLK), jnp.bfloat16),
            pltpu.VMEM((4, 8, ROWS, BLK), jnp.float32),
            pltpu.VMEM((4, 2, 8, HALF, BLK), jnp.bfloat16),
            pltpu.VMEM((2, 4, 8, HALF, BLK), jnp.bfloat16),
            dma((28,)), dma((3,)), dma((3,)), dma((3, 4)), dma((3, 4)), dma((3, NK)), dma((3, NK)),
            dma((4, 3, 2, 2)), dma((4, 3, 2, 2)), dma((3, 2, 4)), dma((2, 4)), dma((2, 2, 4)), dma((4, 2)), dma((2, 4)),
        ],
        compiler_params=pltpu.CompilerParams(collective_id=0, has_side_effects=True, vmem_limit_bytes=56 * 2**20),
        cost_estimate=pl.CostEstimate(flops=17_200_000_000, bytes_accessed=8_000_000, transcendentals=0),
    )(left_size, right_size, left_charge, right_charge, psi, left_ops, right_ops)
    return result[:, None]


def solution(mesh):
    in_specs = (P("sec", None, None, None), P("op", "sec", None, None), P("op", "sec", None, None), P(), P(), P(), P())
    return jax.shard_map(per_device, mesh=mesh, in_specs=in_specs, out_specs=P(None, "sec", "op", None), check_vma=False)
```

```python
import jax
import jax.numpy as jnp
from jax import lax
from jax.experimental import pallas as pl
from jax.experimental.pallas import tpu as pltpu
from jax.sharding import PartitionSpec as P

MESH = pl.DeviceIdType.MESH
BLK = 256
NK = 8
ROWS = 64
HALF = 32


def wrap(i):
    return lax.rem(i, 4)


def kernel(lsize, rsize, lcharge, rcharge, psi, left, right, out,
           lb, rb, pb, pm, inner, stage, far, near, fin, got,
           own_sem, p_send, p_recv, px_send, px_recv, r_send, r_recv, l_send, l_recv,
           x_send, far_recv, x_recv, f_send, f_recv):
    op, sec = lax.axis_index("op"), lax.axis_index("sec")
    x, c = lax.div(op, 2), lax.rem(op, 2)
    z, y = lax.div(sec, 4), lax.rem(sec, 4)
    p, q = y + c * (z - y), z + c * (y - z)

    def sec_at(pp, qq):
        return 4 * qq + pp + 3 * c * (pp - qq)

    def dev(dx=0, dp=0, dq=0, other=False):
        core = 1 - c if other else c
        return (2 * wrap(x + dx) + core, sec_at(wrap(p + dp), wrap(q + dq)))

    def remote(src, dst, send, recv, to):
        return pltpu.make_async_remote_copy(src_ref=src, dst_ref=dst, send_sem=send, recv_sem=recv, device_id=to, device_id_type=MESH)

    barrier = pltpu.get_barrier_semaphore()
    senders = [dev(dp=s) for s in (1, 2, 3)] + [dev(dq=s) for s in (1, 2, 3)] + [dev(dx=s) for s in (1, 3)]
    senders += [dev(dp=s, other=True) for s in range(4)]
    for to in senders:
        pl.semaphore_signal(barrier, 1, device_id=to, device_id_type=MESH)

    def start_row(j, half):
        place = (wrap(x + 2) * ROWS + HALF * half, wrap(x + 1 + 2 * half) * ROWS + HALF * (1 - half), wrap(x + 1 + 2 * half) * ROWS + HALF * half, x * ROWS + HALF * half)[j]
        return pl.ds(pl.multiple_of(place, HALF), HALF)

    def half_rows(half):
        return pl.ds(HALF * half, HALF)

    own = [pltpu.make_async_copy(psi.at[:, sec_at(p, wrap(q + r))], pb.at[r, pl.ds(0, 2)], own_sem.at[r]) for r in range(4)]
    own += [pltpu.make_async_copy(right.at[k, 0], rb.at[0, :, pl.ds(k * BLK, BLK)], own_sem.at[4 + k]) for k in range(NK)]
    for j in range(4):
        for a in range(2):
            for h in range(2):
                own.append(pltpu.make_async_copy(left.at[:, a, start_row(j, h)], lb.at[j, a, :, half_rows(h)], own_sem.at[12 + 4 * j + 2 * a + h]))
    for copy in own:
        copy.start()

    pl.semaphore_wait(barrier, len(senders))

    sent = []

    def start(copy):
        copy.start()
        sent.append(copy)

    def p_copy(s):
        return remote(psi.at[:, sec_at(wrap(p + s), wrap(q + x))], pb.at[x, pl.ds(2 * (4 - s), 2)], p_send.at[s - 1], p_recv.at[3 - s], dev(dp=s))

    def r_copy(k, to_right):
        return remote(right.at[k, 0], rb.at[3 if to_right else 1, :, pl.ds(k * BLK, BLK)],
                      r_send.at[0 if to_right else 1, k], r_recv.at[2 if to_right else 0, k], dev(dq=1 if to_right else 3))

    def r_pass(k):
        here = rb.at[3 if k < 4 else 1, :, pl.ds(k * BLK, BLK)]
        return remote(here, rb.at[2, :, pl.ds(k * BLK, BLK)], r_send.at[2, k], r_recv.at[1, k], dev(dq=1 if k < 4 else 3))

    def l_copy(j, a, h, to_right):
        slot = 3 if to_right else 1
        return remote(left.at[:, a, start_row(j, h)], lb.at[j, 2 * slot + a, :, half_rows(h)],
                      l_send.at[j, 0 if to_right else 1, a, h], l_recv.at[j, slot - 1, a, h], dev(dp=1 if to_right else 3))

    def l_pass(j, a, piece):
        pair = pl.ds(2 * piece, 2)
        here = lb.at[j, 2 * (3 if a == 0 else 1) + a, pair]
        return remote(here, lb.at[j, 4 + a, pair], l_send.at[j, 2, a, piece], l_recv.at[j, 1, a, piece], dev(dp=1 if a == 0 else 3))

    def l_start(j):
        for i in range(2):
            for h in range(2):
                start(l_copy(j, i, h, True))
                start(l_copy(j, 1 - i, h, False))

    def l_forward(j):
        for i in range(2):
            for h in range(2):
                l_copy(j, i, h, True).wait_recv()
            if i == 0:
                for piece in range(4):
                    start(l_pass(j, 0, piece))
            for h in range(2):
                l_copy(j, 1 - i, h, False).wait_recv()
            if i == 0:
                for piece in range(4):
                    start(l_pass(j, 1, piece))

    def px_view(slot_x, piece):
        return pb.at[wrap(x + slot_x), pl.ds((2, 6, 4, 5)[piece], 2 if piece < 2 else 1)]

    def px_copy(piece, to_right):
        return remote(px_view(0, piece), px_view(0, piece), px_send.at[0 if to_right else 1, piece], px_recv.at[2 if to_right else 0, piece],
                      dev(dx=1 if to_right else 3))

    def px_pass(piece):
        slot_x = 3 if piece % 2 == 0 else 1
        return remote(px_view(slot_x, piece), px_view(slot_x, piece), px_send.at[2, piece], px_recv.at[1, piece], dev(dx=1 if piece % 2 == 0 else 3))

    def px_arrive(slot_x, piece):
        return remote(px_view(slot_x, piece), px_view(slot_x, piece), px_send.at[2, piece], px_recv.at[slot_x - 1, piece], dev(dx=1))

    row_at = lax.broadcasted_iota(jnp.int32, (BLK, BLK), 0)
    col_at = lax.broadcasted_iota(jnp.int32, (BLK, BLK), 1)

    def mask_slot(d):
        lax.fori_loop(2, 8, lambda sa, _: mask_block(wrap(x + d), sa), 0)

    def mask_own():
        lax.fori_loop(0, 8, lambda n, _: mask_block(lax.div(n, 2), lax.rem(n, 2)), 0)

    def mask_block(r, sa):
        a = 2 * sec_at(wrap(p + lax.div(sa, 2)), q) + lax.rem(sa, 2)
        b = sec_at(p, wrap(q + r))
        live = (row_at < lsize[a]) & (col_at < rsize[b])
        block = pb[r, sa].astype(jnp.float32)
        pm[r, sa] = jnp.where(live, block, 0.0).astype(jnp.bfloat16)
        return 0

    def slot_order(n):
        return n + lax.div(n, 2) * (5 - 2 * n)

    def far_order(n):
        power = 1 + 3 * x + lax.div(9 * x * (x - 1), 2) + lax.div(27 * x * (x - 1) * (x - 2), 6)
        return lax.rem(lax.div((212, 49, 171, 78)[n], power), 4)

    def first(j, sectors, begin=0, end=4):
        def step(n, _):
            r = wrap(x + slot_order(n))
            for sa in sectors:
                lhs = lb[j, sa].reshape(NK * ROWS, BLK)
                part = jnp.dot(lhs, pm[r, sa], preferred_element_type=jnp.float32).astype(jnp.bfloat16)
                for k in range(NK):
                    inner[r, sa * ROWS:(sa + 1) * ROWS, k * BLK:(k + 1) * BLK] = part[k * ROWS:(k + 1) * ROWS]
            return 0

        steps = end - begin
        lax.fori_loop(begin, end, step, 0, unroll=steps if steps < 4 or len(sectors) < 4 else 2)

    def product(r):
        total = lax.dot_general(inner[r], rb[r], (((1,), (1,)), ((), ())), preferred_element_type=jnp.float32)
        return total.reshape(8, ROWS, BLK)

    def far_copy(side, r):
        return remote(stage.at[0, side, r], far.at[side, r], x_send.at[0, side, r], far_recv.at[side, r], dev(dx=(1, 3)[side]))

    def x_copy(j, side, r):
        return remote(stage.at[j, side, r], near.at[j - 1, side, r], x_send.at[j, side, r], x_recv.at[j - 1, side, r], dev(dx=(1, 3)[side]))

    def fin_copy(r, other):
        core = 1 - c if other else c
        return remote(fin.at[r, core], got.at[c, wrap(4 - r)], f_send.at[r, 1 if other else 0], f_recv.at[c, wrap(4 - r)], dev(dq=r, other=other))

    def halves(total):
        return total[:, :HALF], total[:, HALF:]

    def stage_far(r):
        for side, part in enumerate(halves(product(r))):
            stage[0, side, r] = part.astype(jnp.bfloat16)
            far_copy(side, r).start()

    def stage_one(r):
        for side, part in enumerate(halves(product(r))):
            stage[1, side, r] = part.astype(jnp.bfloat16)
            x_copy(1, side, r).start()

    def stage_two(r):
        parts = halves(product(r))
        for side in range(2):
            far_copy(side, r).wait_recv()
            stage[2, side, r] = (parts[side] + far[side, r].astype(jnp.float32)).astype(jnp.bfloat16)
            x_copy(2, side, r).start()

    def stage_own(r):
        parts = halves(product(r))
        for h in range(2):
            x_copy(2 - h, 0, r).wait_recv()
            x_copy(1 + h, 1, r).wait_recv()
            total = parts[h] + near[1 - h, 0, r].astype(jnp.float32) + near[h, 1, r].astype(jnp.float32)
            fin[r, h] = total.astype(jnp.bfloat16)
        fin_copy(r, True).start()

        @pl.when(r > 0)
        def _():
            fin_copy(r, False).start()

    def run(body, low, high, down=False):
        def step(n, _):
            body(3 - n if down else wrap(x + slot_order(n)))
            return 0

        lax.fori_loop(low, high, step, 0, unroll=2 if (high - low) % 2 == 0 else 1)

    for s in (1, 3, 2):
        start(p_copy(s))
    for copy in own:
        copy.wait()
    mask_own()
    first(0, (0, 1))
    for s in (1, 3):
        p_copy(s).wait_recv()
    for piece in range(2):
        start(px_copy(piece, True))
        start(px_copy(1 - piece, False))
    for i in range(NK):
        start(r_copy(i, True))
        start(r_copy(NK - 1 - i, False))
    p_copy(2).wait_recv()
    for piece in range(2, 4):
        start(px_copy(piece, True))
        start(px_copy(5 - piece, False))
    mask_slot(0)
    for i in range(4):
        r_copy(i, True).wait_recv()
        start(r_pass(i))
        r_copy(NK - 1 - i, False).wait_recv()
        start(r_pass(NK - 1 - i))
    l_start(0)
    for piece in (0, 1):
        px_arrive(3 - 2 * (piece % 2), piece).wait_recv()
        start(px_pass(piece))
    for piece in (2, 3):
        px_arrive(3 - 2 * (piece % 2), piece).wait_recv()
        start(px_pass(piece))
    for i in range(4, NK):
        r_copy(i, True).wait_recv()
        r_copy(NK - 1 - i, False).wait_recv()
    l_forward(0)
    l_start(1)
    for piece in range(4):
        px_arrive(1 + 2 * (piece % 2), piece).wait_recv()
    mask_slot(1)
    mask_slot(3)
    first(0, (2, 3, 6, 7), 0, 3)
    for piece in range(4):
        l_pass(0, 0, piece).wait_recv()
        l_pass(0, 1, piece).wait_recv()
    first(0, (4, 5), 0, 3)
    for n in (0, 1):
        stage_far(far_order(n))
    for k in range(NK):
        r_pass(k).wait_recv()
    l_forward(1)
    l_start(2)
    for piece in range(4):
        px_arrive(2, piece).wait_recv()
    mask_slot(2)
    first(0, range(2, 8), 3, 4)
    for n in (2, 3):
        stage_far(far_order(n))
    first(1, (0, 1, 2, 3, 6, 7))
    for piece in range(4):
        l_pass(1, 0, piece).wait_recv()
        l_pass(1, 1, piece).wait_recv()
    first(1, (4, 5))
    l_forward(2)
    l_start(3)
    run(stage_one, 0, 4)
    first(2, (0, 1, 2, 3, 6, 7))
    for piece in range(4):
        l_pass(2, 0, piece).wait_recv()
        l_pass(2, 1, piece).wait_recv()
    first(2, (4, 5))
    l_forward(3)
    run(stage_two, 0, 4, True)
    first(3, (0, 1, 2, 3, 6, 7))
    for piece in range(4):
        l_pass(3, 0, piece).wait_recv()
        l_pass(3, 1, piece).wait_recv()
    first(3, (4, 5))
    run(stage_own, 0, 4, True)

    got[c, 0] = fin[0, c]

    for copy in sent:
        copy.wait_send()

    def drain(r, _):
        for side in range(2):
            far_copy(side, r).wait_send()
            x_copy(1, side, r).wait_send()
            x_copy(2, side, r).wait_send()
        return 0

    lax.fori_loop(0, 4, drain, 0)

    def arrived(part, slot):
        return remote(fin.at[0, 0], got.at[part, slot], f_send.at[0, 0], f_recv.at[part, slot], dev(dq=1))

    for s in range(4):
        arrived(1 - c, s).wait_recv()
    for s in range(1, 4):
        arrived(c, s).wait_recv()

    row_at = lax.broadcasted_iota(jnp.int32, (32, BLK), 0) + 32 * op
    col_live = lax.broadcasted_iota(jnp.int32, (32, BLK), 1) < rsize[sec]

    def finish(n, _):
        sz, sy, i = lax.div(n, 8), lax.rem(lax.div(n, 2), 4), lax.rem(n, 2)
        a = 2 * (4 * wrap(z + sz) + wrap(y + sy)) + i
        total = got[0, sz, 2 * sy + i].astype(jnp.float32) + got[1, sy, 2 * sz + i].astype(jnp.float32)
        rows = jnp.where(jnp.abs(lcharge[a] - rcharge[sec]) <= 1, lsize[a], 0)
        out[a] = jnp.where((row_at < rows) & col_live, total, 0.0).astype(jnp.bfloat16)
        return 0

    lax.fori_loop(0, 32, finish, 0, unroll=4)

    for r in range(4):
        fin_copy(r, True).wait_send()
    for r in range(1, 4):
        fin_copy(r, False).wait_send()


def per_device(psi, left_ops, right_ops, left_size, right_size, left_charge, right_charge):
    smem = pl.BlockSpec(memory_space=pltpu.SMEM)
    hbm = pl.BlockSpec(memory_space=pl.ANY)
    dma = pltpu.SemaphoreType.DMA
    result = pl.pallas_call(
        kernel,
        out_shape=jax.ShapeDtypeStruct((32, 32, BLK), jnp.bfloat16),
        in_specs=[smem] * 4 + [hbm] * 3,
        out_specs=pl.BlockSpec(memory_space=pltpu.VMEM),
        scratch_shapes=[
            pltpu.VMEM((4, 8, NK, ROWS, BLK), jnp.bfloat16),
            pltpu.VMEM((4, BLK, NK * BLK), jnp.bfloat16),
            pltpu.VMEM((4, 8, BLK, BLK), jnp.bfloat16),
            pltpu.VMEM((4, 8, BLK, BLK), jnp.bfloat16),
            pltpu.VMEM((4, 8 * ROWS, NK * BLK), jnp.bfloat16),
            pltpu.VMEM((3, 2, 4, 8, HALF, BLK), jnp.bfloat16),
            pltpu.VMEM((2, 4, 8, HALF, BLK), jnp.bfloat16),
            pltpu.VMEM((2, 2, 4, 8, HALF, BLK), jnp.bfloat16),
            pltpu.VMEM((4, 2, 8, HALF, BLK), jnp.bfloat16),
            pltpu.VMEM((2, 4, 8, HALF, BLK), jnp.bfloat16),
            dma((28,)), dma((3,)), dma((3,)), dma((3, 4)), dma((3, 4)), dma((3, NK)), dma((3, NK)),
            dma((4, 3, 2, 4)), dma((4, 3, 2, 4)), dma((3, 2, 4)), dma((2, 4)), dma((2, 2, 4)), dma((4, 2)), dma((2, 4)),
        ],
        compiler_params=pltpu.CompilerParams(collective_id=0, has_side_effects=True, vmem_limit_bytes=56 * 2**20),
        cost_estimate=pl.CostEstimate(flops=17_200_000_000, bytes_accessed=8_000_000, transcendentals=0),
    )(left_size, right_size, left_charge, right_charge, psi, left_ops, right_ops)
    return result[:, None]


def solution(mesh):
    in_specs = (P("sec", None, None, None), P("op", "sec", None, None), P("op", "sec", None, None), P(), P(), P(), P())
    return jax.shard_map(per_device, mesh=mesh, in_specs=in_specs, out_specs=P(None, "sec", "op", None), check_vma=False)
```

```python
import jax
import jax.numpy as jnp
from jax import lax
from jax.experimental import pallas as pl
from jax.experimental.pallas import tpu as pltpu
from jax.sharding import PartitionSpec as P

MESH = pl.DeviceIdType.MESH
BLK = 256
NK = 8
BAND = 64
ROWS = 32
HALF = 16


def wrap(i):
    return lax.rem(i, 4)


def kernel(lsize, rsize, lcharge, rcharge, psi, left, right, out,
           lb, rb, pb, pm, inner, stage, far, near, fin, got,
           own_sem, p_send, p_recv, px_send, px_recv, r_send, r_recv, l_send, l_recv,
           x_send, far_recv, x_recv, f_send, f_recv):
    op, sec = lax.axis_index("op"), lax.axis_index("sec")
    x, c = lax.div(op, 2), lax.rem(op, 2)
    z, y = lax.div(sec, 4), lax.rem(sec, 4)
    p, q = y + c * (z - y), z + c * (y - z)

    def sec_at(pp, qq):
        return 4 * qq + pp + 3 * c * (pp - qq)

    def dev(dx=0, dp=0, dq=0, other=False):
        core = 1 - c if other else c
        return (2 * wrap(x + dx) + core, sec_at(wrap(p + dp), wrap(q + dq)))

    def remote(src, dst, send, recv, to):
        return pltpu.make_async_remote_copy(src_ref=src, dst_ref=dst, send_sem=send, recv_sem=recv, device_id=to, device_id_type=MESH)

    barrier = pltpu.get_barrier_semaphore()
    senders = [dev(dp=s) for s in (1, 2, 3)] + [dev(dq=s) for s in (1, 2, 3)] + [dev(dx=s) for s in (1, 3)]
    senders += [dev(dp=s, other=True) for s in range(4)]
    for to in senders:
        pl.semaphore_signal(barrier, 1, device_id=to, device_id_type=MESH)

    def start_row(j, half):
        kind, sub = j // 2, j % 2
        place = (wrap(x + 2) * BAND + 32 * half, wrap(x + 1 + 2 * half) * BAND + 32 * (1 - half), wrap(x + 1 + 2 * half) * BAND + 32 * half, x * BAND + 32 * half)[kind]
        return pl.ds(pl.multiple_of(place + HALF * sub, HALF), HALF)

    def half_rows(half):
        return pl.ds(HALF * half, HALF)

    own = [pltpu.make_async_copy(psi.at[:, sec_at(p, wrap(q + r))], pb.at[r, pl.ds(0, 2)], own_sem.at[r]) for r in range(4)]
    own += [pltpu.make_async_copy(right.at[k, 0], rb.at[0, :, pl.ds(k * BLK, BLK)], own_sem.at[4 + k]) for k in range(NK)]
    for j in range(8):
        for a in range(2):
            for h in range(2):
                own.append(pltpu.make_async_copy(left.at[:, a, start_row(j, h)], lb.at[j, a, :, half_rows(h)], own_sem.at[12 + 4 * j + 2 * a + h]))
    for copy in own:
        copy.start()

    pl.semaphore_wait(barrier, len(senders))

    sent = []

    def start(copy):
        copy.start()
        sent.append(copy)

    def p_copy(s):
        return remote(psi.at[:, sec_at(wrap(p + s), wrap(q + x))], pb.at[x, pl.ds(2 * (4 - s), 2)], p_send.at[s - 1], p_recv.at[3 - s], dev(dp=s))

    def r_copy(k, to_right):
        return remote(right.at[k, 0], rb.at[3 if to_right else 1, :, pl.ds(k * BLK, BLK)],
                      r_send.at[0 if to_right else 1, k], r_recv.at[2 if to_right else 0, k], dev(dq=1 if to_right else 3))

    def r_pass(k):
        here = rb.at[3 if k < 4 else 1, :, pl.ds(k * BLK, BLK)]
        return remote(here, rb.at[2, :, pl.ds(k * BLK, BLK)], r_send.at[2, k], r_recv.at[1, k], dev(dq=1 if k < 4 else 3))

    def l_copy(j, a, h, to_right):
        slot = 3 if to_right else 1
        return remote(left.at[:, a, start_row(j, h)], lb.at[j, 2 * slot + a, :, half_rows(h)],
                      l_send.at[j, 0 if to_right else 1, a, h], l_recv.at[j, slot - 1, a, h], dev(dp=1 if to_right else 3))

    def l_pass(j, a, piece):
        pair = pl.ds(4 * piece, 4)
        here = lb.at[j, 2 * (3 if a == 0 else 1) + a, pair]
        return remote(here, lb.at[j, 4 + a, pair], l_send.at[j, 2, a, piece], l_recv.at[j, 1, a, piece], dev(dp=1 if a == 0 else 3))

    def l_start(j):
        for i in range(2):
            for h in range(2):
                start(l_copy(j, i, h, True))
                start(l_copy(j, 1 - i, h, False))

    def l_forward(j):
        for i in range(2):
            for h in range(2):
                l_copy(j, i, h, True).wait_recv()
            if i == 0:
                for piece in range(2):
                    start(l_pass(j, 0, piece))
            for h in range(2):
                l_copy(j, 1 - i, h, False).wait_recv()
            if i == 0:
                for piece in range(2):
                    start(l_pass(j, 1, piece))

    def px_view(slot_x, piece):
        return pb.at[wrap(x + slot_x), pl.ds((2, 6, 4, 5)[piece], 2 if piece < 2 else 1)]

    def px_copy(piece, to_right):
        return remote(px_view(0, piece), px_view(0, piece), px_send.at[0 if to_right else 1, piece], px_recv.at[2 if to_right else 0, piece],
                      dev(dx=1 if to_right else 3))

    def px_pass(piece):
        slot_x = 3 if piece % 2 == 0 else 1
        return remote(px_view(slot_x, piece), px_view(slot_x, piece), px_send.at[2, piece], px_recv.at[1, piece], dev(dx=1 if piece % 2 == 0 else 3))

    def px_arrive(slot_x, piece):
        return remote(px_view(slot_x, piece), px_view(slot_x, piece), px_send.at[2, piece], px_recv.at[slot_x - 1, piece], dev(dx=1))

    row_at = lax.broadcasted_iota(jnp.int32, (BLK, BLK), 0)
    col_at = lax.broadcasted_iota(jnp.int32, (BLK, BLK), 1)

    def mask_slot(d):
        lax.fori_loop(2, 8, lambda sa, _: mask_block(wrap(x + d), sa), 0)

    def mask_own():
        lax.fori_loop(0, 8, lambda n, _: mask_block(lax.div(n, 2), lax.rem(n, 2)), 0)

    def mask_block(r, sa):
        a = 2 * sec_at(wrap(p + lax.div(sa, 2)), q) + lax.rem(sa, 2)
        b = sec_at(p, wrap(q + r))
        live = (row_at < lsize[a]) & (col_at < rsize[b])
        block = pb[r, sa].astype(jnp.float32)
        pm[r, sa] = jnp.where(live, block, 0.0).astype(jnp.bfloat16)
        return 0

    def slot_order(n):
        return n + lax.div(n, 2) * (5 - 2 * n)

    def far_order(n):
        power = 1 + 3 * x + lax.div(9 * x * (x - 1), 2) + lax.div(27 * x * (x - 1) * (x - 2), 6)
        return lax.rem(lax.div((212, 49, 171, 78)[n], power), 4)

    def first(j, many, sectors, begin=0, end=4):
        def step(n, _):
            r = wrap(x + slot_order(n))
            for sa in sectors:
                lhs = lb[j:j + many, sa].reshape(many * NK * ROWS, BLK)
                part = jnp.dot(lhs, pm[r, sa], preferred_element_type=jnp.float32).astype(jnp.bfloat16)
                for sub in range(many):
                    for k in range(NK):
                        at = (sub * NK + k) * ROWS
                        inner[r, sub, sa * ROWS:(sa + 1) * ROWS, k * BLK:(k + 1) * BLK] = part[at:at + ROWS]
            return 0

        steps = end - begin
        lax.fori_loop(begin, end, step, 0, unroll=2 if many == 2 and len(sectors) > 2 else steps)

    def product(r, many):
        lhs = inner[r, :many].reshape(many * 8 * ROWS, NK * BLK)
        total = lax.dot_general(lhs, rb[r], (((1,), (1,)), ((), ())), preferred_element_type=jnp.float32)
        return total.reshape(many, 8, ROWS, BLK)

    def far_copy(sub, side, r):
        return remote(stage.at[sub, side, r], far.at[sub, side, r], x_send.at[sub, side, r], far_recv.at[sub, side, r], dev(dx=(1, 3)[side]))

    def x_copy(kind, sub, side, r):
        j = 2 * kind + sub
        return remote(stage.at[j, side, r], near.at[j - 2, side, r], x_send.at[j, side, r], x_recv.at[j - 2, side, r], dev(dx=(1, 3)[side]))

    def fin_copy(r, other):
        core = 1 - c if other else c
        return remote(fin.at[r, core], got.at[c, wrap(4 - r)], f_send.at[r, 1 if other else 0], f_recv.at[c, wrap(4 - r)], dev(dq=r, other=other))

    def halves(total):
        return total[:, :HALF], total[:, HALF:]

    def stage_far(r, sub):
        for side, part in enumerate(halves(product(r, 1)[0])):
            stage[sub, side, r] = part.astype(jnp.bfloat16)
            far_copy(sub, side, r).start()

    def stage_one(r, _):
        total = product(r, 2)
        for sub in range(2):
            for side, part in enumerate(halves(total[sub])):
                stage[2 + sub, side, r] = part.astype(jnp.bfloat16)
                x_copy(1, sub, side, r).start()

    def stage_two(r, _):
        total = product(r, 2)
        for sub in range(2):
            for side, part in enumerate(halves(total[sub])):
                far_copy(sub, side, r).wait_recv()
                stage[4 + sub, side, r] = (part + far[sub, side, r].astype(jnp.float32)).astype(jnp.bfloat16)
                x_copy(2, sub, side, r).start()

    def stage_own(r, _):
        total = product(r, 2)
        for sub in range(2):
            for h, part in enumerate(halves(total[sub])):
                x_copy(2 - h, sub, 0, r).wait_recv()
                x_copy(1 + h, sub, 1, r).wait_recv()
                part = part + near[2 * (1 - h) + sub, 0, r].astype(jnp.float32) + near[2 * h + sub, 1, r].astype(jnp.float32)
                fin[r, h, :, HALF * sub:HALF * (sub + 1)] = part.astype(jnp.bfloat16)
        fin_copy(r, True).start()

        @pl.when(r > 0)
        def _():
            fin_copy(r, False).start()

    def run(body, low, high, sub, down=False):
        def step(n, _):
            r = 3 - n if down else wrap(x + slot_order(n))
            body(r, sub)
            return 0

        lax.fori_loop(low, high, step, 0, unroll=2)

    for s in (1, 3, 2):
        start(p_copy(s))
    for copy in own:
        copy.wait()
    mask_own()
    first(0, 1, (0, 1))
    for s in (1, 3):
        p_copy(s).wait_recv()
    for piece in range(2):
        start(px_copy(piece, True))
        start(px_copy(1 - piece, False))
    for i in range(NK):
        start(r_copy(i, True))
        start(r_copy(NK - 1 - i, False))
    p_copy(2).wait_recv()
    for piece in range(2, 4):
        start(px_copy(piece, True))
        start(px_copy(5 - piece, False))
    mask_slot(0)
    for i in range(4):
        r_copy(i, True).wait_recv()
        start(r_pass(i))
        r_copy(NK - 1 - i, False).wait_recv()
        start(r_pass(NK - 1 - i))
    l_start(0)
    l_start(1)
    for piece in (0, 1):
        px_arrive(3 - 2 * (piece % 2), piece).wait_recv()
        start(px_pass(piece))
    for piece in (2, 3):
        px_arrive(3 - 2 * (piece % 2), piece).wait_recv()
        start(px_pass(piece))
    for i in range(4, NK):
        r_copy(i, True).wait_recv()
        r_copy(NK - 1 - i, False).wait_recv()
    l_forward(0)
    l_start(2)
    for piece in range(4):
        px_arrive(1 + 2 * (piece % 2), piece).wait_recv()
    mask_slot(1)
    mask_slot(3)
    first(0, 1, (2, 3, 6, 7), 0, 3)
    for piece in range(2):
        l_pass(0, 0, piece).wait_recv()
        l_pass(0, 1, piece).wait_recv()
    first(0, 1, (4, 5), 0, 3)
    l_forward(1)
    l_start(3)
    for n in (0, 1):
        stage_far(far_order(n), 0)
    for k in range(NK):
        r_pass(k).wait_recv()
    for piece in range(4):
        px_arrive(2, piece).wait_recv()
    mask_slot(2)
    first(0, 1, range(2, 8), 3, 4)
    for n in (2, 3):
        stage_far(far_order(n), 0)
    l_forward(2)
    l_start(4)
    first(1, 1, (0, 1, 2, 3, 6, 7))
    for piece in range(2):
        l_pass(1, 0, piece).wait_recv()
        l_pass(1, 1, piece).wait_recv()
    first(1, 1, (4, 5))
    l_forward(3)
    l_start(5)
    run(stage_far, 0, 4, 1)
    first(2, 2, (0, 1, 2, 3, 6, 7))
    for piece in range(2):
        l_pass(2, 0, piece).wait_recv()
        l_pass(2, 1, piece).wait_recv()
    for piece in range(2):
        l_pass(3, 0, piece).wait_recv()
        l_pass(3, 1, piece).wait_recv()
    l_forward(4)
    l_start(6)
    first(2, 2, (4, 5))
    run(stage_one, 0, 4, 0)
    l_forward(5)
    l_start(7)
    first(4, 2, (0, 1, 2, 3, 6, 7))
    for piece in range(2):
        l_pass(4, 0, piece).wait_recv()
        l_pass(4, 1, piece).wait_recv()
    for piece in range(2):
        l_pass(5, 0, piece).wait_recv()
        l_pass(5, 1, piece).wait_recv()
    l_forward(6)
    first(4, 2, (4, 5))
    run(stage_two, 0, 4, 0, True)
    l_forward(7)
    first(6, 2, (0, 1, 2, 3, 6, 7))
    for piece in range(2):
        l_pass(6, 0, piece).wait_recv()
        l_pass(6, 1, piece).wait_recv()
    for piece in range(2):
        l_pass(7, 0, piece).wait_recv()
        l_pass(7, 1, piece).wait_recv()
    first(6, 2, (4, 5))
    run(stage_own, 0, 4, 0, True)

    got[c, 0] = fin[0, c]

    for copy in sent:
        copy.wait_send()

    def drain(r, _):
        for side in range(2):
            for sub in range(2):
                far_copy(sub, side, r).wait_send()
                x_copy(1, sub, side, r).wait_send()
                x_copy(2, sub, side, r).wait_send()
        return 0

    lax.fori_loop(0, 4, drain, 0)

    def arrived(part, slot):
        return remote(fin.at[0, 0], got.at[part, slot], f_send.at[0, 0], f_recv.at[part, slot], dev(dq=1))

    for s in range(4):
        arrived(1 - c, s).wait_recv()
    for s in range(1, 4):
        arrived(c, s).wait_recv()

    row_at = lax.broadcasted_iota(jnp.int32, (32, BLK), 0) + 32 * op
    col_live = lax.broadcasted_iota(jnp.int32, (32, BLK), 1) < rsize[sec]

    def finish(n, _):
        sz, sy, i = lax.div(n, 8), lax.rem(lax.div(n, 2), 4), lax.rem(n, 2)
        a = 2 * (4 * wrap(z + sz) + wrap(y + sy)) + i
        total = got[0, sz, 2 * sy + i].astype(jnp.float32) + got[1, sy, 2 * sz + i].astype(jnp.float32)
        rows = jnp.where(jnp.abs(lcharge[a] - rcharge[sec]) <= 1, lsize[a], 0)
        out[a] = jnp.where((row_at < rows) & col_live, total, 0.0).astype(jnp.bfloat16)
        return 0

    lax.fori_loop(0, 32, finish, 0)

    for r in range(4):
        fin_copy(r, True).wait_send()
    for r in range(1, 4):
        fin_copy(r, False).wait_send()


def per_device(psi, left_ops, right_ops, left_size, right_size, left_charge, right_charge):
    smem = pl.BlockSpec(memory_space=pltpu.SMEM)
    hbm = pl.BlockSpec(memory_space=pl.ANY)
    dma = pltpu.SemaphoreType.DMA
    result = pl.pallas_call(
        kernel,
        out_shape=jax.ShapeDtypeStruct((32, 32, BLK), jnp.bfloat16),
        in_specs=[smem] * 4 + [hbm] * 3,
        out_specs=pl.BlockSpec(memory_space=pltpu.VMEM),
        scratch_shapes=[
            pltpu.VMEM((8, 8, NK, ROWS, BLK), jnp.bfloat16),
            pltpu.VMEM((4, BLK, NK * BLK), jnp.bfloat16),
            pltpu.VMEM((4, 8, BLK, BLK), jnp.bfloat16),
            pltpu.VMEM((4, 8, BLK, BLK), jnp.bfloat16),
            pltpu.VMEM((4, 2, 8 * ROWS, NK * BLK), jnp.bfloat16),
            pltpu.VMEM((6, 2, 4, 8, HALF, BLK), jnp.bfloat16),
            pltpu.VMEM((2, 2, 4, 8, HALF, BLK), jnp.bfloat16),
            pltpu.VMEM((4, 2, 4, 8, HALF, BLK), jnp.bfloat16),
            pltpu.VMEM((4, 2, 8, 32, BLK), jnp.bfloat16),
            pltpu.VMEM((2, 4, 8, 32, BLK), jnp.bfloat16),
            dma((44,)), dma((3,)), dma((3,)), dma((3, 4)), dma((3, 4)), dma((3, NK)), dma((3, NK)),
            dma((8, 3, 2, 2)), dma((8, 3, 2, 2)), dma((6, 2, 4)), dma((2, 2, 4)), dma((4, 2, 4)), dma((4, 2)), dma((2, 4)),
        ],
        compiler_params=pltpu.CompilerParams(collective_id=0, has_side_effects=True, vmem_limit_bytes=56 * 2**20),
        cost_estimate=pl.CostEstimate(flops=17_200_000_000, bytes_accessed=8_000_000, transcendentals=0),
    )(left_size, right_size, left_charge, right_charge, psi, left_ops, right_ops)
    return result[:, None]


def solution(mesh):
    in_specs = (P("sec", None, None, None), P("op", "sec", None, None), P("op", "sec", None, None), P(), P(), P(), P())
    return jax.shard_map(per_device, mesh=mesh, in_specs=in_specs, out_specs=P(None, "sec", "op", None), check_vma=False)
```
